32 devices in a mesh: row: 4 (over z), col: 8 (over y, x, core).
Axes of the slice: x: 2, y: 2, z: 4, core: 2. Of those that a mesh axis runs over, the one named last changes fastest.
Arguments:
- patches: bfloat16 [24576, 1536], P(('row', 'col')), may hold values from -6 to 6
- dest: int32 [24576], P(('row', 'col')), may hold values from -1 to 511, as said below
- background: bfloat16 [1536], replicated, may hold values from -6 to 6
- conv_weight: float32 [7, 7, 1536], replicated, may hold values from -0.875 to 0.875
- conv_bias: float32 [1536], replicated, may hold values from -3 to 3
- norm_gain: float32 [1536], replicated, may hold values from 0.1 to 1.9
- norm_bias: float32 [1536], replicated, may hold values from -3 to 3
- w_in: bfloat16 [6144, 1536], P('col'), may hold values from -0.15625 to 0.15625
- b_in: bfloat16 [6144], P('col'), may hold values from -3 to 3
- w_out: bfloat16 [6144, 1536], P('col'), may hold values from -0.078125 to 0.078125
- b_out: float32 [1536], replicated, may hold values from -3 to 3
- layer_scale: float32 [1536], replicated, may hold values from 0.3 to 1.5
Outputs:
- features: bfloat16 [128, 128, 1536], P('row', 'col')
The draws below stay inside these ranges and needn't reach their ends.
Inputs may be any that keep to these rules, and one draw needn't show every extreme that they name: `dest`: -1 marks an empty slot; no cell is named twice among all slots sent to one device; in every draw some device fills all 96 slots it sends to some device, and some device receives a patch for every one of its cells.
All inputs are finite; a program needn't handle non-finite values.
Results may differ from the reference program's by a relative error of at most 0.0046.
Values may be sent and summed in bfloat16 or wider, within the bound.
A program may use at most 128 MiB of HBM per device.

```python
import math
import jax
import jax.numpy as jnp
from jax import lax

C = 1536
FF = 6144
TH = 32
TW = 16
NR = 128
NC = 128
CAP = 96
ROUTE_ROWS = 24576
N_ROW = 4
N_COL = 8


def draw_dest(key, part):
    cells = TH * TW
    slots = N_COL * CAP
    receivers = N_ROW * N_COL
    key_cells, key_slots, key_full, key_count = jax.random.split(key, 4)
    cell_order = jax.vmap(lambda k: jax.random.permutation(k, cells))(jax.random.split(key_cells, receivers))
    slot_order = jax.vmap(lambda k: jax.random.permutation(k, slots))(jax.random.split(key_slots, receivers))
    full_sender = jax.random.randint(key_full, (receivers,), 0, N_COL)
    sender_of_slot = jnp.arange(slots) // CAP
    scores = jnp.where(sender_of_slot[None, :] == full_sender[:, None], slot_order - 2 * slots, slot_order)
    order = jnp.argsort(scores, axis=1, stable=True)
    ranking = jnp.argsort(order, axis=1, stable=True)
    count = jnp.minimum(jax.random.randint(key_count, (receivers,), cells // 2, cells + cells // 4 + 1), cells)
    picked = jnp.take_along_axis(cell_order, jnp.minimum(ranking, cells - 1), axis=1)
    result = jnp.where(ranking < count[:, None], picked, -1)
    result = result.reshape(N_ROW, N_COL, N_COL, CAP).transpose(0, 2, 1, 3)
    return result.reshape(-1).astype(jnp.int32)


def level_of(rng, shape, pieces, low, high):
    def one(dim, blocks):
        steps = jax.random.uniform(jax.random.fold_in(jax.random.fold_in(rng, 6), dim), (blocks,), jnp.float32, low / len(pieces), high / len(pieces))
        return jnp.repeat(jnp.exp(steps), shape[dim] // blocks).reshape((-1,) + (1,) * (len(shape) - dim - 1))

    loudness = one(*pieces[0])
    for cut in pieces[1:]:
        loudness = loudness * one(*cut)
    return loudness


def noise(rng, shape, scale, reach, pieces=(), kind=jnp.bfloat16):
    values = jax.random.normal(rng, shape, jnp.float32) * scale
    if len(pieces) > 0:
        values = level_of(rng, shape, pieces, -0.22, 0.18) * values
    return jnp.clip(values, min=-reach, max=reach).astype(kind)


def setup_inputs(seed: int = 0) -> dict:
    arg_keys = jax.random.split(jax.random.key(seed), 13)
    return {
        "patches": noise(arg_keys[0], (ROUTE_ROWS, C), 1.0, 6.0, ((0, 32),)),
        "dest": draw_dest(jax.random.fold_in(arg_keys[12], 71), 0),
        "background": noise(arg_keys[2], (C,), 1.0, 6.0),
        "conv_weight": noise(arg_keys[3], (7, 7, C), 49 ** -0.5, 0.875, (), jnp.float32),
        "conv_bias": noise(arg_keys[4], (C,), 0.5, 3.0, (), jnp.float32),
        "norm_gain": jnp.clip(1.0 + 0.18 * jax.random.normal(arg_keys[5], (C,), jnp.float32), 0.1, 1.9),
        "norm_bias": noise(arg_keys[6], (C,), 0.5, 3.0, (), jnp.float32),
        "w_in": noise(arg_keys[7], (FF, C), C ** -0.5, 0.15625, ((0, 8),)),
        "b_in": noise(arg_keys[8], (FF,), 0.5, 3.0, ((0, 8),)),
        "w_out": noise(arg_keys[9], (FF, C), FF ** -0.5, 0.078125, ((0, 8),)),
        "b_out": noise(arg_keys[10], (C,), 0.5, 3.0, (), jnp.float32),
        "layer_scale": jnp.clip(jnp.exp(jax.random.uniform(arg_keys[11], (C,), jnp.float32, math.log(0.3), math.log(1.5))), 0.3, 1.5),
    }


def reference(patches, dest, background, conv_weight, conv_bias, norm_gain, norm_bias, w_in, b_in, w_out, b_out, layer_scale):
    slot = dest.reshape(N_ROW, N_COL, N_COL, CAP)
    row_ids = jnp.arange(N_ROW, dtype=jnp.int32)[:, None, None, None]
    recv_ids = jnp.arange(N_COL, dtype=jnp.int32)[None, None, :, None]
    grid_row = row_ids * TH + slot // TW
    grid_col = recv_ids * TW + slot % TW
    flat_index = jnp.where(slot >= 0, grid_row * NC + grid_col, NR * NC).reshape(-1).astype(jnp.int32)
    canvas = jnp.zeros((NR * NC, C), jnp.bfloat16).at[flat_index].set(patches, mode='drop')
    filled = jnp.zeros((NR * NC,), jnp.int32).at[flat_index].set(1, mode='drop')
    grid = jnp.where(filled[:, None] > 0, canvas, background[None, :]).reshape(NR, NC, C)
    padded = jnp.pad(grid.astype(jnp.float32), ((3, 3), (3, 3), (0, 0)))
    conv = jnp.zeros((NR, NC, C), jnp.float32) + conv_bias
    for across in range(7):
        for along in range(7):
            conv = conv + padded[across:across + NR, along:along + NC, :] * conv_weight[across, along]
    mean = lax.optimization_barrier(jnp.mean(conv, axis=-1, keepdims=True))
    centred = conv - mean
    var = lax.optimization_barrier(jnp.mean(centred * centred, axis=-1, keepdims=True))
    normed = (centred * lax.rsqrt(var + 1e-06) * norm_gain + norm_bias).astype(jnp.bfloat16)

    def pointwise(rows):
        pre = jnp.dot(rows, w_in.T, preferred_element_type=jnp.float32) + b_in.astype(jnp.float32)
        hidden = jax.nn.gelu(pre, approximate=False).astype(jnp.bfloat16)
        return jnp.dot(hidden, w_out, preferred_element_type=jnp.float32)
    mixed = lax.map(pointwise, normed)
    out = grid.astype(jnp.float32) + layer_scale * (mixed + b_out)
    return out.astype(jnp.bfloat16)
```

```python
import jax
import jax.numpy as jnp
from jax import lax
from jax.sharding import PartitionSpec as P

TH = 32
TW = 16


def extended(cells, sides, width):
    for axis, dim in sides:
        count = lax.axis_size(axis)
        ends = count - 1
        head = lax.slice_in_dim(cells, 0, width, axis=dim)
        tail = lax.slice_in_dim(cells, cells.shape[dim] - width, cells.shape[dim], axis=dim)
        cells = jnp.concatenate(
            [
                lax.ppermute(tail, axis, [(i, (i + 1) % count) for i in range(ends)]),
                cells,
                lax.ppermute(head, axis, [((i + 1) % count, i) for i in range(ends)]),
            ],
            axis=dim,
        )
    return cells


def expand(rows, weight_rows, bias_rows):
    pre = lax.dot_general(
        rows, weight_rows, (((1,), (1,)), ((), ())), preferred_element_type=jnp.float32
    )
    return jax.nn.gelu(pre + bias_rows.astype(jnp.float32), approximate=False).astype(jnp.bfloat16)


def mlp(rows, weight_in, bias, weight_out):
    return jnp.dot(
        expand(rows, weight_in, bias), weight_out, preferred_element_type=jnp.float32
    )


def local(
    patches,
    dest,
    background,
    conv_weight,
    conv_bias,
    norm_gain,
    norm_bias,
    w_in,
    b_in,
    w_out,
    b_out,
    layer_scale,
):
    cells = TH * TW
    channels = patches.shape[1]
    count = lax.axis_size("col")
    lines = count // 4
    mates = [(i, i ^ 1) for i in range(count)]
    sides = [(i, i ^ 2) for i in range(count)]
    second = tuple(lax.ppermute(part, "col", sides) for part in (w_in, b_in, w_out))
    moved, moved_dest = (
        lax.all_to_all(patches, "col", split_axis=0, concat_axis=0, tiled=True),
        lax.all_to_all(dest, "col", split_axis=0, concat_axis=0, tiled=True),
    )
    cell_ids = jnp.arange(cells, dtype=jnp.int32)
    onehot = moved_dest[None, :] == cell_ids[:, None]
    placed = jnp.dot(onehot.astype(jnp.bfloat16), moved, preferred_element_type=jnp.float32)
    present = jnp.any(onehot, axis=1)
    grid = jnp.where(present[:, None], placed, background.astype(jnp.float32)[None, :]).astype(
        jnp.bfloat16
    )
    grid_block = grid.reshape(TH, TW, channels)
    padded = extended(grid_block, (("row", 0), ("col", 1)), 3)
    conv = jnp.zeros((TH, TW, channels), jnp.float32) + conv_bias
    for across in range(7):
        for along in range(7):
            conv = (
                conv
                + padded[across : across + TH, along : along + TW, :].astype(jnp.float32)
                * conv_weight[across, along]
            )
    mean = jnp.mean(conv, axis=-1, keepdims=True)
    centred = conv - mean
    var = jnp.mean(centred * centred, axis=-1, keepdims=True)
    normed = (centred * lax.rsqrt(var + 1e-06) * norm_gain + norm_bias).astype(jnp.bfloat16)
    flat = normed.reshape(cells, channels)
    home, mate = flat, lax.ppermute(flat, "col", mates)
    away = []
    for step in range(1, lines):
        there = lax.ppermute(flat, "col", [(i, (i + 4 * step) % count) for i in range(count)])
        away.append((there, lax.ppermute(there, "col", mates)))
    first = (w_in, b_in, w_out)
    near, far = [mlp(home, *first), mlp(mate, *first)], []
    for there, cross in away:
        far.append([mlp(cross, *first), mlp(there, *first)])
    back = []
    for step, (there, cross) in enumerate(away, 1):
        lent = (far[step - 1][0] + mlp(cross, *second)).astype(jnp.bfloat16)
        lent = lax.ppermute(lent, "col", mates)
        total = far[step - 1][1] + mlp(there, *second) + lent.astype(jnp.float32)
        back.append(
            lax.ppermute(
                total.astype(jnp.bfloat16),
                "col",
                [((i + 4 * step) % count, i) for i in range(count)],
            )
        )
    lent = lax.ppermute((near[1] + mlp(mate, *second)).astype(jnp.bfloat16), "col", mates)
    mixed = near[0] + mlp(home, *second) + lent.astype(jnp.float32)
    for part in back:
        mixed = mixed + part.astype(jnp.float32)
    result = grid.astype(jnp.float32) + layer_scale * (mixed + b_out)
    return result.astype(jnp.bfloat16).reshape(TH, TW, channels)


def solution(mesh):
    placed = (
        P(("row", "col"), None),
        P(("row", "col")),
        P(),
        P(),
        P(),
        P(),
        P(),
        P("col", None),
        P("col"),
        P("col", None),
        P(),
        P(),
    )
    return jax.shard_map(
        local, mesh=mesh, in_specs=placed, out_specs=P("row", "col", None), check_vma=False
    )
```

```python
import jax
import jax.numpy as jnp
from jax import lax
from jax.sharding import PartitionSpec as P

TH = 32
TW = 16


def extended(cells, sides, width):
    for axis, dim in sides:
        count = lax.axis_size(axis)
        ends = count - 1
        head = lax.slice_in_dim(cells, 0, width, axis=dim)
        tail = lax.slice_in_dim(cells, cells.shape[dim] - width, cells.shape[dim], axis=dim)
        cells = jnp.concatenate(
            [
                lax.ppermute(tail, axis, [(i, (i + 1) % count) for i in range(ends)]),
                cells,
                lax.ppermute(head, axis, [((i + 1) % count, i) for i in range(ends)]),
            ],
            axis=dim,
        )
    return cells


def expand(rows, weight_rows, bias_rows):
    pre = lax.dot_general(
        rows, weight_rows, (((1,), (1,)), ((), ())), preferred_element_type=jnp.float32
    )
    return jax.nn.gelu(pre + bias_rows.astype(jnp.float32), approximate=False).astype(jnp.bfloat16)


def local(
    patches,
    dest,
    background,
    conv_weight,
    conv_bias,
    norm_gain,
    norm_bias,
    w_in,
    b_in,
    w_out,
    b_out,
    layer_scale,
):
    cells = TH * TW
    channels = patches.shape[1]
    count = lax.axis_size("col")
    chips = count // 2
    mates = [(i, i ^ 1) for i in range(count)]
    groups = [[2 * chip + core for chip in range(chips)] for core in range(2)]
    some_in, some_out = (
        lax.all_gather(part, "col", axis=0, tiled=True, axis_index_groups=groups)
        for part in (w_in, w_out)
    )
    shifted = [b_in] + [
        lax.ppermute(b_in, "col", [(i, (i + 2 * step) % count) for i in range(count)])
        for step in range(1, chips)
    ]
    order = jnp.remainder(lax.axis_index("col") // 2 - jnp.arange(chips), chips)
    some_bias = jnp.take(jnp.stack(shifted), order, axis=0).reshape(-1)
    moved, moved_dest = (
        lax.all_to_all(patches, "col", split_axis=0, concat_axis=0, tiled=True),
        lax.all_to_all(dest, "col", split_axis=0, concat_axis=0, tiled=True),
    )
    cell_ids = jnp.arange(cells, dtype=jnp.int32)
    onehot = moved_dest[None, :] == cell_ids[:, None]
    placed = jnp.dot(onehot.astype(jnp.bfloat16), moved, preferred_element_type=jnp.float32)
    present = jnp.any(onehot, axis=1)
    grid = jnp.where(present[:, None], placed, background.astype(jnp.float32)[None, :]).astype(
        jnp.bfloat16
    )
    grid_block = grid.reshape(TH, TW, channels)
    padded = extended(grid_block, (("row", 0), ("col", 1)), 3)
    conv = jnp.zeros((TH, TW, channels), jnp.float32) + conv_bias
    for across in range(7):
        for along in range(7):
            conv = (
                conv
                + padded[across : across + TH, along : along + TW, :].astype(jnp.float32)
                * conv_weight[across, along]
            )
    mean = jnp.mean(conv, axis=-1, keepdims=True)
    centred = conv - mean
    var = jnp.mean(centred * centred, axis=-1, keepdims=True)
    normed = (centred * lax.rsqrt(var + 1e-06) * norm_gain + norm_bias).astype(jnp.bfloat16)
    flat = normed.reshape(cells, channels)
    mate = lax.ppermute(flat, "col", mates)
    home_hidden = lax.optimization_barrier(expand(flat, some_in, some_bias))
    mate_hidden = lax.optimization_barrier(expand(mate, some_in, some_bias))
    lent = jnp.dot(mate_hidden, some_out, preferred_element_type=jnp.float32).astype(jnp.bfloat16)
    lent = lax.ppermute(lent, "col", mates)
    mixed = jnp.dot(home_hidden, some_out, preferred_element_type=jnp.float32)
    mixed = mixed + lent.astype(jnp.float32)
    result = grid.astype(jnp.float32) + layer_scale * (mixed + b_out)
    return result.astype(jnp.bfloat16).reshape(TH, TW, channels)


def solution(mesh):
    placed = (
        P(("row", "col"), None),
        P(("row", "col")),
        P(),
        P(),
        P(),
        P(),
        P(),
        P("col", None),
        P("col"),
        P("col", None),
        P(),
        P(),
    )
    return jax.shard_map(
        local, mesh=mesh, in_specs=placed, out_specs=P("row", "col", None), check_vma=False
    )
```

```python
import jax
import jax.numpy as jnp
from jax import lax
from jax.sharding import PartitionSpec as P

TH = 32
TW = 16


def extended(cells, sides, width):
    for axis, dim in sides:
        count = lax.axis_size(axis)
        ends = count - 1
        head = lax.slice_in_dim(cells, 0, width, axis=dim)
        tail = lax.slice_in_dim(cells, cells.shape[dim] - width, cells.shape[dim], axis=dim)
        cells = jnp.concatenate(
            [
                lax.ppermute(tail, axis, [(i, (i + 1) % count) for i in range(ends)]),
                cells,
                lax.ppermute(head, axis, [((i + 1) % count, i) for i in range(ends)]),
            ],
            axis=dim,
        )
    return cells


def expand(rows, weight_rows, bias_rows):
    pre = lax.dot_general(
        rows, weight_rows, (((1,), (1,)), ((), ())), preferred_element_type=jnp.float32
    )
    return jax.nn.gelu(pre + bias_rows.astype(jnp.float32), approximate=False).astype(jnp.bfloat16)


def mlp(rows, weight_in, bias, weight_out):
    hidden = lax.optimization_barrier(expand(rows, weight_in, bias))
    return jnp.dot(hidden, weight_out, preferred_element_type=jnp.float32)


def local(
    patches,
    dest,
    background,
    conv_weight,
    conv_bias,
    norm_gain,
    norm_bias,
    w_in,
    b_in,
    w_out,
    b_out,
    layer_scale,
):
    cells = TH * TW
    channels = patches.shape[1]
    count = lax.axis_size("col")
    lines = count // 4
    mates = [(i, i ^ 1) for i in range(count)]
    sides = [(i, i ^ 2) for i in range(count)]
    groups = [[i, i ^ 2] for i in range(count) if i % 4 < 2]
    pair_in, pair_out = (
        lax.all_gather(part, "col", axis=0, tiled=True, axis_index_groups=groups)
        for part in (w_in, w_out)
    )
    other = lax.ppermute(b_in, "col", sides)
    low = lax.axis_index("col") % 4 < 2
    pair_bias = jnp.concatenate([jnp.where(low, b_in, other), jnp.where(low, other, b_in)])
    pair = (pair_in, pair_bias, pair_out)
    moved, moved_dest = (
        lax.all_to_all(patches, "col", split_axis=0, concat_axis=0, tiled=True),
        lax.all_to_all(dest, "col", split_axis=0, concat_axis=0, tiled=True),
    )
    cell_ids = jnp.arange(cells, dtype=jnp.int32)
    onehot = moved_dest[None, :] == cell_ids[:, None]
    placed = jnp.dot(onehot.astype(jnp.bfloat16), moved, preferred_element_type=jnp.float32)
    present = jnp.any(onehot, axis=1)
    grid = jnp.where(present[:, None], placed, background.astype(jnp.float32)[None, :]).astype(
        jnp.bfloat16
    )
    grid_block = grid.reshape(TH, TW, channels)
    padded = extended(grid_block, (("row", 0), ("col", 1)), 3)
    conv = jnp.zeros((TH, TW, channels), jnp.float32) + conv_bias
    for across in range(7):
        for along in range(7):
            conv = (
                conv
                + padded[across : across + TH, along : along + TW, :].astype(jnp.float32)
                * conv_weight[across, along]
            )
    mean = jnp.mean(conv, axis=-1, keepdims=True)
    centred = conv - mean
    var = jnp.mean(centred * centred, axis=-1, keepdims=True)
    normed = (centred * lax.rsqrt(var + 1e-06) * norm_gain + norm_bias).astype(jnp.bfloat16)
    flat = normed.reshape(cells, channels)
    home, mate = flat, lax.ppermute(flat, "col", mates)
    away = []
    for step in range(1, lines):
        there = lax.ppermute(flat, "col", [(i, (i + 4 * step) % count) for i in range(count)])
        away.append((there, lax.ppermute(there, "col", mates)))
    near = [mlp(home, *pair), mlp(mate, *pair)]
    back = []
    for step, (there, cross) in enumerate(away, 1):
        lent = mlp(cross, *pair).astype(jnp.bfloat16)
        lent = lax.ppermute(lent, "col", mates)
        total = mlp(there, *pair) + lent.astype(jnp.float32)
        back.append(
            lax.ppermute(
                total.astype(jnp.bfloat16),
                "col",
                [((i + 4 * step) % count, i) for i in range(count)],
            )
        )
    lent = lax.ppermute(near[1].astype(jnp.bfloat16), "col", mates)
    mixed = near[0] + lent.astype(jnp.float32)
    for part in back:
        mixed = mixed + part.astype(jnp.float32)
    result = grid.astype(jnp.float32) + layer_scale * (mixed + b_out)
    return result.astype(jnp.bfloat16).reshape(TH, TW, channels)


def solution(mesh):
    placed = (
        P(("row", "col"), None),
        P(("row", "col")),
        P(),
        P(),
        P(),
        P(),
        P(),
        P("col", None),
        P("col"),
        P("col", None),
        P(),
        P(),
    )
    return jax.shard_map(
        local, mesh=mesh, in_specs=placed, out_specs=P("row", "col", None), check_vma=False
    )
```

```python
import jax
import jax.numpy as jnp
from jax import lax
from jax.sharding import PartitionSpec as P

TH = 32
TW = 16


def extended(cells, sides, width):
    for axis, dim in sides:
        count = lax.axis_size(axis)
        ends = count - 1
        head = lax.slice_in_dim(cells, 0, width, axis=dim)
        tail = lax.slice_in_dim(cells, cells.shape[dim] - width, cells.shape[dim], axis=dim)
        cells = jnp.concatenate(
            [
                lax.ppermute(tail, axis, [(i, (i + 1) % count) for i in range(ends)]),
                cells,
                lax.ppermute(head, axis, [((i + 1) % count, i) for i in range(ends)]),
            ],
            axis=dim,
        )
    return cells


def expand(rows, weight_rows, bias_rows):
    pre = lax.dot_general(
        rows, weight_rows, (((1,), (1,)), ((), ())), preferred_element_type=jnp.float32
    )
    return jax.nn.gelu(pre + bias_rows.astype(jnp.float32), approximate=False).astype(jnp.bfloat16)


def mlp(rows, weight_in, bias, weight_out):
    hidden = lax.optimization_barrier(expand(rows, weight_in, bias))
    return jnp.dot(hidden, weight_out, preferred_element_type=jnp.float32)


def local(
    patches,
    dest,
    background,
    conv_weight,
    conv_bias,
    norm_gain,
    norm_bias,
    w_in,
    b_in,
    w_out,
    b_out,
    layer_scale,
):
    cells = TH * TW
    channels = patches.shape[1]
    count = lax.axis_size("col")
    lines = count // 4
    mates = [(i, i ^ 1) for i in range(count)]
    sides = [(i, i ^ 2) for i in range(count)]
    groups = [[i, i ^ 2] for i in range(count) if i % 4 < 2]
    pair_in, pair_out = lax.all_gather(
        jnp.stack([w_in, w_out]), "col", axis=1, tiled=True, axis_index_groups=groups
    )
    other = lax.ppermute(b_in, "col", sides)
    low = lax.axis_index("col") % 4 < 2
    pair_bias = jnp.concatenate([jnp.where(low, b_in, other), jnp.where(low, other, b_in)])
    pair = (pair_in, pair_bias, pair_out)
    moved, moved_dest = (
        lax.all_to_all(patches, "col", split_axis=0, concat_axis=0, tiled=True),
        lax.all_to_all(dest, "col", split_axis=0, concat_axis=0, tiled=True),
    )
    cell_ids = jnp.arange(cells, dtype=jnp.int32)
    onehot = moved_dest[None, :] == cell_ids[:, None]
    placed = jnp.dot(onehot.astype(jnp.bfloat16), moved, preferred_element_type=jnp.float32)
    present = jnp.any(onehot, axis=1)
    grid = jnp.where(present[:, None], placed, background.astype(jnp.float32)[None, :]).astype(
        jnp.bfloat16
    )
    grid_block = grid.reshape(TH, TW, channels)
    padded = extended(grid_block, (("row", 0), ("col", 1)), 3)
    conv = jnp.zeros((TH, TW, channels), jnp.float32) + conv_bias
    for across in range(7):
        for along in range(7):
            conv = (
                conv
                + padded[across : across + TH, along : along + TW, :].astype(jnp.float32)
                * conv_weight[across, along]
            )
    mean = jnp.mean(conv, axis=-1, keepdims=True)
    centred = conv - mean
    var = jnp.mean(centred * centred, axis=-1, keepdims=True)
    normed = (centred * lax.rsqrt(var + 1e-06) * norm_gain + norm_bias).astype(jnp.bfloat16)
    flat = normed.reshape(cells, channels)
    home, mate = flat, lax.ppermute(flat, "col", mates)
    near = [mlp(home, *pair)]
    away = []
    for step in range(1, lines):
        there = lax.ppermute(flat, "col", [(i, (i + 4 * step) % count) for i in range(count)])
        there, near[0] = lax.optimization_barrier((there, near[0]))
        away.append((there, lax.ppermute(there, "col", mates)))
    near.append(mlp(mate, *pair))
    back = []
    for step, (there, cross) in enumerate(away, 1):
        lent = mlp(cross, *pair).astype(jnp.bfloat16)
        lent = lax.ppermute(lent, "col", mates)
        total = mlp(there, *pair) + lent.astype(jnp.float32)
        back.append(
            lax.ppermute(
                total.astype(jnp.bfloat16),
                "col",
                [((i + 4 * step) % count, i) for i in range(count)],
            )
        )
    lent = lax.ppermute(near[1].astype(jnp.bfloat16), "col", mates)
    mixed = near[0] + lent.astype(jnp.float32)
    for part in back:
        mixed = mixed + part.astype(jnp.float32)
    result = grid.astype(jnp.float32) + layer_scale * (mixed + b_out)
    return result.astype(jnp.bfloat16).reshape(TH, TW, channels)


def solution(mesh):
    placed = (
        P(("row", "col"), None),
        P(("row", "col")),
        P(),
        P(),
        P(),
        P(),
        P(),
        P("col", None),
        P("col"),
        P("col", None),
        P(),
        P(),
    )
    return jax.shard_map(
        local, mesh=mesh, in_specs=placed, out_specs=P("row", "col", None), check_vma=False
    )
```

```python
import jax
import jax.numpy as jnp
from jax import lax
from jax.sharding import PartitionSpec as P

TH = 32
TW = 16


def extended(cells, sides, width):
    for axis, dim in sides:
        count = lax.axis_size(axis)
        ends = count - 1
        head = lax.slice_in_dim(cells, 0, width, axis=dim)
        tail = lax.slice_in_dim(cells, cells.shape[dim] - width, cells.shape[dim], axis=dim)
        cells = jnp.concatenate(
            [
                lax.ppermute(tail, axis, [(i, (i + 1) % count) for i in range(ends)]),
                cells,
                lax.ppermute(head, axis, [((i + 1) % count, i) for i in range(ends)]),
            ],
            axis=dim,
        )
    return cells


def expand(rows, weight_rows, bias_rows):
    pre = lax.dot_general(
        rows, weight_rows, (((1,), (1,)), ((), ())), preferred_element_type=jnp.float32
    )
    return jax.nn.gelu(pre + bias_rows.astype(jnp.float32), approximate=False).astype(jnp.bfloat16)


def mlp(rows, weight_in, bias, weight_out):
    hidden = lax.optimization_barrier(expand(rows, weight_in, bias))
    return jnp.dot(hidden, weight_out, preferred_element_type=jnp.float32)


def local(
    patches,
    dest,
    background,
    conv_weight,
    conv_bias,
    norm_gain,
    norm_bias,
    w_in,
    b_in,
    w_out,
    b_out,
    layer_scale,
):
    cells = TH * TW
    channels = patches.shape[1]
    count = lax.axis_size("col")
    lines = count // 4
    mates = [(i, i ^ 1) for i in range(count)]
    sides = [(i, i ^ 2) for i in range(count)]
    groups = [[i, i ^ 2] for i in range(count) if i % 4 < 2]
    pair_in, pair_out = lax.all_gather(
        jnp.stack([w_in, w_out]), "col", axis=1, tiled=True, axis_index_groups=groups
    )
    other = lax.ppermute(b_in, "col", sides)
    low = lax.axis_index("col") % 4 < 2
    pair_bias = jnp.concatenate([jnp.where(low, b_in, other), jnp.where(low, other, b_in)])
    pair = (pair_in, pair_bias, pair_out)
    moved, moved_dest = (
        lax.all_to_all(patches, "col", split_axis=0, concat_axis=0, tiled=True),
        lax.all_to_all(dest, "col", split_axis=0, concat_axis=0, tiled=True),
    )
    cell_ids = jnp.arange(cells, dtype=jnp.int32)
    onehot = moved_dest[None, :] == cell_ids[:, None]
    placed = jnp.dot(onehot.astype(jnp.bfloat16), moved, preferred_element_type=jnp.float32)
    present = jnp.any(onehot, axis=1)
    grid = jnp.where(present[:, None], placed, background.astype(jnp.float32)[None, :]).astype(
        jnp.bfloat16
    )
    grid_block = grid.reshape(TH, TW, channels)
    padded = extended(grid_block, (("row", 0), ("col", 1)), 3)
    conv = jnp.zeros((TH, TW, channels), jnp.float32) + conv_bias
    for across in range(7):
        for along in range(7):
            conv = (
                conv
                + padded[across : across + TH, along : along + TW, :].astype(jnp.float32)
                * conv_weight[across, along]
            )
    mean = jnp.mean(conv, axis=-1, keepdims=True)
    centred = conv - mean
    var = jnp.mean(centred * centred, axis=-1, keepdims=True)
    normed = (centred * lax.rsqrt(var + 1e-06) * norm_gain + norm_bias).astype(jnp.bfloat16)
    flat = normed.reshape(cells, channels)
    home, mate = flat, lax.ppermute(flat, "col", mates)
    away = []
    for step in range(1, lines):
        there = lax.ppermute(flat, "col", [(i, (i + 4 * step) % count) for i in range(count)])
        away.append((there, lax.ppermute(there, "col", mates)))
    near = mlp(mate, *pair)
    back = []
    for step, (there, cross) in enumerate(away, 1):
        lent = mlp(cross, *pair).astype(jnp.bfloat16)
        lent = lax.ppermute(lent, "col", mates)
        total = mlp(there, *pair) + lent.astype(jnp.float32)
        total, home = lax.optimization_barrier((total.astype(jnp.bfloat16), home))
        back.append(
            lax.ppermute(
                total,
                "col",
                [((i + 4 * step) % count, i) for i in range(count)],
            )
        )
    lent = lax.ppermute(near.astype(jnp.bfloat16), "col", mates)
    mixed = mlp(home, *pair) + lent.astype(jnp.float32)
    for part in back:
        mixed = mixed + part.astype(jnp.float32)
    result = grid.astype(jnp.float32) + layer_scale * (mixed + b_out)
    return result.astype(jnp.bfloat16).reshape(TH, TW, channels)


def solution(mesh):
    placed = (
        P(("row", "col"), None),
        P(("row", "col")),
        P(),
        P(),
        P(),
        P(),
        P(),
        P("col", None),
        P("col"),
        P("col", None),
        P(),
        P(),
    )
    return jax.shard_map(
        local, mesh=mesh, in_specs=placed, out_specs=P("row", "col", None), check_vma=False
    )
```

```python
import jax
import jax.numpy as jnp
from jax import lax
from jax.sharding import PartitionSpec as P

TH = 32
TW = 16


def extended(cells, sides, width):
    for axis, dim in sides:
        count = lax.axis_size(axis)
        ends = count - 1
        head = lax.slice_in_dim(cells, 0, width, axis=dim)
        tail = lax.slice_in_dim(cells, cells.shape[dim] - width, cells.shape[dim], axis=dim)
        cells = jnp.concatenate(
            [
                lax.ppermute(tail, axis, [(i, (i + 1) % count) for i in range(ends)]),
                cells,
                lax.ppermute(head, axis, [((i + 1) % count, i) for i in range(ends)]),
            ],
            axis=dim,
        )
    return cells


def expand(rows, weight_rows, bias_rows):
    pre = lax.dot_general(
        rows, weight_rows, (((1,), (1,)), ((), ())), preferred_element_type=jnp.float32
    )
    return jax.nn.gelu(pre + bias_rows.astype(jnp.float32), approximate=False).astype(jnp.bfloat16)


def mlp(rows, weight_in, bias, weight_out):
    hidden = lax.optimization_barrier(expand(rows, weight_in, bias))
    return jnp.dot(hidden, weight_out, preferred_element_type=jnp.float32)


def local(
    patches,
    dest,
    background,
    conv_weight,
    conv_bias,
    norm_gain,
    norm_bias,
    w_in,
    b_in,
    w_out,
    b_out,
    layer_scale,
):
    cells = TH * TW
    channels = patches.shape[1]
    count = lax.axis_size("col")
    lines = count // 4
    mates = [(i, i ^ 1) for i in range(count)]
    sides = [(i, i ^ 2) for i in range(count)]
    groups = [[i, i ^ 2] for i in range(count) if i % 4 < 2]
    pair_in, pair_out = (
        lax.all_gather(part, "col", axis=0, tiled=True, axis_index_groups=groups)
        for part in (w_in, w_out)
    )
    other = lax.ppermute(b_in, "col", sides)
    low = lax.axis_index("col") % 4 < 2
    pair_bias = jnp.concatenate([jnp.where(low, b_in, other), jnp.where(low, other, b_in)])
    pair = (pair_in, pair_bias, pair_out)
    moved, moved_dest = (
        lax.all_to_all(patches, "col", split_axis=0, concat_axis=0, tiled=True),
        lax.all_to_all(dest, "col", split_axis=0, concat_axis=0, tiled=True),
    )
    cell_ids = jnp.arange(cells, dtype=jnp.int32)
    onehot = moved_dest[None, :] == cell_ids[:, None]
    placed = jnp.dot(onehot.astype(jnp.bfloat16), moved, preferred_element_type=jnp.float32)
    present = jnp.any(onehot, axis=1)
    grid = jnp.where(present[:, None], placed, background.astype(jnp.float32)[None, :]).astype(
        jnp.bfloat16
    )
    grid_block = grid.reshape(TH, TW, channels)
    padded = extended(grid_block, (("row", 0), ("col", 1)), 3)
    conv = jnp.zeros((TH, TW, channels), jnp.float32) + conv_bias
    for across in range(7):
        for along in range(7):
            conv = (
                conv
                + padded[across : across + TH, along : along + TW, :].astype(jnp.float32)
                * conv_weight[across, along]
            )
    mean = jnp.mean(conv, axis=-1, keepdims=True)
    centred = conv - mean
    var = jnp.mean(centred * centred, axis=-1, keepdims=True)
    normed = (centred * lax.rsqrt(var + 1e-06) * norm_gain + norm_bias).astype(jnp.bfloat16)
    flat = normed.reshape(cells, channels)
    home, mate = flat, lax.ppermute(flat, "col", mates)
    away = []
    for step in range(1, lines):
        there = lax.ppermute(flat, "col", [(i, (i + 4 * step) % count) for i in range(count)])
        away.append((there, lax.ppermute(there, "col", mates)))
    near = mlp(mate, *pair)
    back = []
    for step, (there, cross) in enumerate(away, 1):
        lent = mlp(cross, *pair).astype(jnp.bfloat16)
        lent = lax.ppermute(lent, "col", mates)
        total = mlp(there, *pair) + lent.astype(jnp.float32)
        total, home = lax.optimization_barrier((total.astype(jnp.bfloat16), home))
        back.append(
            lax.ppermute(
                total,
                "col",
                [((i + 4 * step) % count, i) for i in range(count)],
            )
        )
    lent = lax.ppermute(near.astype(jnp.bfloat16), "col", mates)
    mixed = mlp(home, *pair) + lent.astype(jnp.float32)
    for part in back:
        mixed = mixed + part.astype(jnp.float32)
    result = grid.astype(jnp.float32) + layer_scale * (mixed + b_out)
    return result.astype(jnp.bfloat16).reshape(TH, TW, channels)


def solution(mesh):
    placed = (
        P(("row", "col"), None),
        P(("row", "col")),
        P(),
        P(),
        P(),
        P(),
        P(),
        P("col", None),
        P("col"),
        P("col", None),
        P(),
        P(),
    )
    return jax.shard_map(
        local, mesh=mesh, in_specs=placed, out_specs=P("row", "col", None), check_vma=False
    )
```
